32 devices in a mesh: chan: 8 (over z, core), freq: 4 (over y, x).
Axes of the slice: x: 2, y: 2, z: 4, core: 2. Of those that a mesh axis runs over, the one named last changes fastest.
Arguments:
- segments: bfloat16 [64, 2048, 1024], P('freq', 'chan'), may hold values from -120 to 120, as said below
- available: int32 [64, 2048], P('freq', 'chan'), may hold values 0 or 1
- node_windows: int32 [4], P('freq'), may hold values from 1 to 16, 40 in all
Outputs:
- cross_stack: bfloat16 [2, 128, 2048, 2048], P(None, 'freq', 'chan')
The draws below stay inside these ranges and needn't reach their ends.
Inputs may be any that keep to these rules, and one draw needn't show every extreme that they name: `segments`: samples are finite and of moderate size. `node_windows`: A node's windows fill its first slots; the counts of all nodes sum to 40.
All inputs are finite; a program needn't handle non-finite values. No bound on the sum of `available` or of `node_windows` on one device may be relied on, other than what follows from the above.
Results may differ from the reference program's by a relative error of at most 0.013.
Values may be sent and summed in bfloat16 or wider, within the bound.
No kernel may reach another device: no remote copies, remote signals or barrier semaphores. Data moves between devices by JAX's collectives and lax.ppermute only.
A program may use at most 448 MiB of HBM per device.

```python
import math
import jax
import jax.numpy as jnp
import numpy as np
from jax import lax

CHANNELS = 2048
FREQS = 128
SAMPLES = 1024
FIRST_BIN = 64
WSLOT = 16
W_ALL = 64
WINDOWS = 40
N_FREQ = 4


def draw_segments(key, part):
    keys = jax.random.split(key, 5)
    shape = (W_ALL, CHANNELS, SAMPLES)
    row_scale = jnp.exp(jax.random.uniform(keys[0], (W_ALL, CHANNELS, 1), jnp.float32, 0.0, math.log(10.0)))
    tone_bin = FIRST_BIN + jax.random.uniform(keys[1], (W_ALL, CHANNELS, 1), jnp.float32) * FREQS
    tone_size = jax.random.uniform(keys[2], (W_ALL, CHANNELS, 1), jnp.float32, 0.5, 3.0)
    tone_shift = jax.random.uniform(keys[3], (W_ALL, CHANNELS, 1), jnp.float32, 0.0, 2.0 * math.pi)
    sample_index = jnp.arange(SAMPLES, dtype=jnp.float32)[None, None, :]
    cycles = tone_bin * sample_index / SAMPLES
    cycles = cycles - jnp.floor(cycles)
    tone = tone_size * jnp.sin(2.0 * math.pi * cycles + tone_shift)
    noise = jax.random.normal(keys[4], shape, jnp.float32)
    noise = jnp.clip(noise, -6.0, 6.0)
    values = row_scale * (noise + tone)
    return values.astype(jnp.bfloat16)


def with_ends(array, own_key, least, largest):
    place = [jax.random.randint(jax.random.fold_in(own_key, axis), (), 0, length) for axis, length in enumerate(array.shape)]
    widest = array.shape.index(max(array.shape))
    neighbour = place[:widest] + [(place[widest] + 1) % array.shape[widest]] + place[widest + 1:]
    return array.at[tuple(place)].set(least).at[tuple(neighbour)].set(largest)


def length_profile(count, total, bound, slope):
    portions = [(1 << 20) // math.isqrt(rank ** slope) + 1 for rank in range(2, count + 1)]
    spare, counts = total - bound - (count - 1), [1] * (count - 1)
    while spare > 0:
        candidates = [i for i in range(count - 1) if counts[i] < bound]
        whole, budget = sum([portions[i] for i in candidates]), spare
        for i in candidates:
            more = min(bound - counts[i], max(1, budget * portions[i] // whole), spare)
            counts[i] = counts[i] + more
            spare = spare - more
    return np.array([bound] + counts)


def ragged(own_key, count, total, limit, skew):
    if count == 2:
        one = jax.random.randint(own_key, (), max(1, total - limit), min(limit, total - 1) + 1)
        return jnp.stack([one, total - one])
    sizes = jnp.asarray(length_profile(count, total, limit, skew), jnp.int32)
    couples = (count - 1) // 2
    donor, sink = sizes[1:1 + 2 * couples:2], sizes[2:2 + 2 * couples:2]
    room = jnp.minimum(donor - 1, limit - sink)
    moved = jax.random.randint(jax.random.fold_in(own_key, 1), (couples,), 0, 1 << 20) % (room + 1)
    sizes = sizes.at[1:1 + 2 * couples:2].set(donor - moved).at[2:2 + 2 * couples:2].set(sink + moved)
    return sizes[jax.random.permutation(jax.random.fold_in(own_key, 2), count)]


def setup_inputs(seed: int = 0) -> dict:
    key_of = jax.random.split(jax.random.key(seed), 4)
    return {
        "segments": draw_segments(jax.random.fold_in(key_of[3], 71), 0),
        "available": with_ends((jax.random.randint(key_of[1], (W_ALL, CHANNELS), 0, 5) < 4).astype(jnp.int32), jax.random.fold_in(key_of[1], 1), 0, 1),
        "node_windows": ragged(key_of[2], N_FREQ, WINDOWS, WSLOT, 2).astype(jnp.int32),
    }


epsilon = 1e-06

def transform_rows(sample_count, bin_count, first_bin):
    sample_index = jnp.arange(sample_count, dtype=jnp.int32)[:, None]
    bin_index = (first_bin + jnp.arange(bin_count, dtype=jnp.int32))[None, :]
    angles = (bin_index * sample_index % sample_count).astype(jnp.float32) * (2.0 * math.pi / sample_count)
    return jnp.concatenate([jnp.cos(angles), -jnp.sin(angles)], axis=1).astype(jnp.bfloat16)

def reference(segments, available, node_windows):
    slot_index = jnp.arange(W_ALL, dtype=jnp.int32)
    node_index = slot_index // WSLOT
    limits = node_windows[node_index]
    live_mask = available * (slot_index % WSLOT < limits).astype(jnp.int32)[:, None]
    cos_sin = transform_rows(SAMPLES, FREQS, FIRST_BIN)
    raw_spectra = jnp.dot(segments.reshape(W_ALL * CHANNELS, SAMPLES), cos_sin, preferred_element_type=jnp.float32)
    raw_spectra = raw_spectra.reshape(W_ALL, CHANNELS, 2, FREQS)
    spectra = (raw_spectra * live_mask.astype(jnp.float32)[:, :, None, None]).astype(jnp.bfloat16)
    spectra_wide = spectra.astype(jnp.float32)
    energy = lax.optimization_barrier(jnp.sum(spectra_wide * spectra_wide, axis=(2, 3))) / FREQS
    whitened = (spectra_wide * lax.rsqrt(energy + epsilon)[:, :, None, None]).astype(jnp.bfloat16)
    by_bin = jnp.transpose(whitened, (3, 2, 0, 1))
    stack_scale = jnp.float32(1.0 / WINDOWS)

    def per_bin(bin_block):
        stacked_rows = bin_block.reshape(2 * W_ALL, CHANNELS)
        flipped = jnp.concatenate([bin_block[1], -bin_block[0]], axis=0)
        real_part = jnp.dot(stacked_rows.T, stacked_rows, preferred_element_type=jnp.float32)
        imag_part = jnp.dot(flipped.T, stacked_rows, preferred_element_type=jnp.float32)
        return (jnp.stack([real_part, imag_part]) * stack_scale).astype(jnp.bfloat16)
    per_freq = lax.map(per_bin, by_bin)
    return jnp.transpose(per_freq, (1, 0, 2, 3))
```

```python
import functools
import math

import jax
import jax.numpy as jnp
import ml_dtypes
import numpy as np
from jax import lax
from jax.experimental import pallas as pl
from jax.experimental.pallas import tpu as pltpu
from jax.sharding import PartitionSpec as P

FREQS = 128
FIRST_BIN = 64
EPSILON = 1e-06
CHUNK_BINS = 8
VMEM_LIMIT = 40 << 20


def transform_table(nodes, chunks, chunk_bins, samples):
    sample_index = np.arange(samples, dtype=np.int64)[None, :]
    bin_index = (FIRST_BIN + np.arange(FREQS, dtype=np.int64))[:, None]
    angles = (bin_index * sample_index % samples).astype(np.float64) * (2.0 * math.pi / samples)
    parts = np.stack([np.cos(angles), -np.sin(angles)]).astype(np.float32).astype(ml_dtypes.bfloat16)
    parts = parts.reshape(2, nodes, chunks, chunk_bins, samples).transpose(1, 2, 0, 3, 4)
    return parts.reshape(nodes, chunks * 2 * chunk_bins, samples)


def spectra_kernel(nodes, chunks, piece_rows, me_ref, count_ref, seg_ref, avail_ref, table_ref, *refs):
    pieces, table = refs[:-1], refs[-1]
    step = pl.program_id(0)
    node_rows = chunks * piece_rows

    @pl.when(step == 0)
    def _():
        for d in range(nodes):
            table[d * node_rows:(d + 1) * node_rows, :] = table_ref[me_ref[0] ^ d]

    block = seg_ref.shape[0]
    for i in range(block):
        w = step * block + i
        raw = lax.dot_general(
            table[...], seg_ref[i], (((1,), (1,)), ((), ())), preferred_element_type=jnp.float32
        )
        live = jnp.where(w < count_ref[0], avail_ref[pl.ds(w, 1), :], 0).astype(jnp.float32)
        spectra = (raw * live).astype(jnp.bfloat16).astype(jnp.float32)
        energy = jnp.sum(spectra * spectra, axis=0, keepdims=True) / FREQS
        whitened = (spectra * lax.rsqrt(energy + EPSILON)).astype(jnp.bfloat16)
        for p, piece in enumerate(pieces):
            piece[w] = whitened[p * piece_rows:(p + 1) * piece_rows]


def spectra_pieces(me, node_windows, segments, available, table, chunks, chunk_bins):
    slots, chan, samples = segments.shape
    nodes = table.shape[0]
    piece = jax.ShapeDtypeStruct((slots, 2 * chunk_bins, chan), jnp.bfloat16)
    block = 2
    out = pl.pallas_call(
        functools.partial(spectra_kernel, nodes, chunks, 2 * chunk_bins),
        grid=(slots // block,),
        in_specs=[
            pl.BlockSpec(memory_space=pltpu.SMEM),
            pl.BlockSpec(memory_space=pltpu.SMEM),
            pl.BlockSpec((block, chan, samples), lambda i: (i, 0, 0)),
            pl.BlockSpec((slots, chan), lambda i: (0, 0)),
            pl.BlockSpec(table.shape, lambda i: (0, 0, 0)),
        ],
        out_specs=[pl.BlockSpec(piece.shape, lambda i: (0, 0, 0))] * (nodes * chunks),
        out_shape=[piece] * (nodes * chunks),
        scratch_shapes=[pltpu.VMEM((2 * FREQS, samples), jnp.bfloat16)],
        compiler_params=pltpu.CompilerParams(vmem_limit_bytes=VMEM_LIMIT),
        cost_estimate=pl.CostEstimate(
            flops=2 * slots * chan * samples * 2 * FREQS, bytes_accessed=2 * slots * chan * samples, transcendentals=0
        ),
        name="spectra",
    )(me, node_windows, segments, available, table)
    return [out[d * chunks:(d + 1) * chunks] for d in range(nodes)]


def pack_kernel(nodes, slots, chunk_bins, windows, me_ref, *refs):
    counts, pieces, (packed_ref, flipped_ref) = refs[:nodes], refs[nodes:2 * nodes], refs[2 * nodes:]
    me = me_ref[0]
    chan = packed_ref.shape[2]
    out_rows, in_rows = chunk_bins * 2 * windows, slots * 2 * chunk_bins
    col = lax.broadcasted_iota(jnp.int32, (1, in_rows), 1)
    slot, part, fbin = col // (2 * chunk_bins), (col // chunk_bins) % 2, col % chunk_bins
    row = lax.broadcasted_iota(jnp.int32, (out_rows, in_rows), 0)
    sign = jnp.where(part == 1, 1.0, -1.0)
    packed = jnp.zeros((out_rows, chan), jnp.float32)
    flipped = jnp.zeros((out_rows, chan), jnp.float32)
    for d in range(nodes):
        start = 0
        for e in range(nodes):
            start = start + jnp.where((me ^ e) < (me ^ d), counts[e][0], 0)
        place = fbin * (2 * windows) + start + slot
        alive = slot < counts[d][0]
        own = jnp.where(alive, place + part * windows, -1)
        other = jnp.where(alive, place + (1 - part) * windows, -1)
        rows = pieces[d][...].reshape(in_rows, chan)
        packed += jnp.dot(
            jnp.where(row == own, 1.0, 0.0).astype(jnp.bfloat16), rows, preferred_element_type=jnp.float32
        )
        flipped += jnp.dot(
            jnp.where(row == other, sign, 0.0).astype(jnp.bfloat16), rows, preferred_element_type=jnp.float32
        )
    packed_ref[...] = packed.astype(jnp.bfloat16).reshape(packed_ref.shape)
    flipped_ref[...] = flipped.astype(jnp.bfloat16).reshape(flipped_ref.shape)


def pack_windows(me, counts, pieces, chunk_bins, windows):
    slots, _, chan = pieces[0].shape
    nodes = len(pieces)
    shape = jax.ShapeDtypeStruct((chunk_bins, 2 * windows, chan), jnp.bfloat16)
    whole = pl.BlockSpec(memory_space=pltpu.VMEM)
    return pl.pallas_call(
        functools.partial(pack_kernel, nodes, slots, chunk_bins, windows),
        in_specs=[pl.BlockSpec(memory_space=pltpu.SMEM)] * (1 + nodes) + [whole] * nodes,
        out_specs=[whole, whole],
        out_shape=[shape, shape],
        compiler_params=pltpu.CompilerParams(vmem_limit_bytes=VMEM_LIMIT),
        cost_estimate=pl.CostEstimate(
            flops=1 << 30, bytes_accessed=1 << 21, transcendentals=0
        ),
        name="pack",
    )(me, *counts, *pieces)


def pairs_kernel(steps, chan, scale, place_ref, flipped_ref, *refs):
    blocks, out_ref = refs[:2 * steps], refs[-1]
    z, core = place_ref[0] // 2, place_ref[0] % 2
    both = jnp.concatenate([blocks[0][0], flipped_ref[0]], axis=1)
    rows = jnp.transpose(both, (1, 0))
    for t in range(steps):
        source = lax.rem(z - t + steps, steps) * 2
        for k in range(2):
            column = (source + (core if k == 0 else 1 - core)) * chan
            product = jnp.dot(rows, blocks[2 * t + k][0], preferred_element_type=jnp.float32) * scale
            product = product.astype(jnp.bfloat16)
            columns = pl.ds(pl.multiple_of(column, chan), chan)
            out_ref[0, 0, :, columns] = product[:chan]
            out_ref[1, 0, :, columns] = product[chan:]


def pair_products(place, flipped, blocks, out, bins, chunk, scale):
    chunk_bins, depth, chan = flipped.shape
    steps = len(blocks) // 2
    total = chan * 2 * steps
    block_spec = pl.BlockSpec((1, depth, chan), lambda i: (i, 0, 0))
    specs = [pl.BlockSpec(memory_space=pltpu.SMEM)] + [block_spec] * (1 + len(blocks))
    operands = [place, flipped, *blocks]
    aliases = {}
    if out is not None:
        specs.append(pl.BlockSpec(memory_space=pl.ANY))
        aliases = {len(operands): 0}
        operands.append(out)
    return pl.pallas_call(
        functools.partial(pairs_kernel, steps, chan, scale),
        grid=(chunk_bins,),
        in_specs=specs,
        out_specs=pl.BlockSpec((2, 1, chan, total), lambda i: (0, chunk * chunk_bins + i, 0, 0)),
        out_shape=jax.ShapeDtypeStruct((2, bins, chan, total), jnp.bfloat16),
        input_output_aliases=aliases,
        compiler_params=pltpu.CompilerParams(vmem_limit_bytes=VMEM_LIMIT),
        cost_estimate=pl.CostEstimate(
            flops=4 * chunk_bins * depth * chan * total,
            bytes_accessed=4 * chunk_bins * chan * total,
            transcendentals=0,
        ),
        name="pairs",
    )(*operands)


def shards(nodes, groups, segments, available, node_windows):
    slots, chan, samples = segments.shape
    bins = FREQS // nodes
    chunk_bins = math.gcd(bins, CHUNK_BINS)
    chunks = bins // chunk_bins
    windows = slots * nodes * 5 // 8
    steps = groups // 2
    me = lax.axis_index("freq").astype(jnp.int32).reshape(1)
    place = lax.axis_index("chan").astype(jnp.int32).reshape(1)
    swap = [[(f, f ^ d) for f in range(nodes)] for d in range(nodes)]
    ring = [(i, (i + 2) % groups) for i in range(groups)]
    cores = [(i, i ^ 1) for i in range(groups)]

    counts = [node_windows] + [lax.ppermute(node_windows, "freq", swap[d]) for d in range(1, nodes)]
    table = jnp.asarray(transform_table(nodes, chunks, chunk_bins, samples))
    pieces = spectra_pieces(me, node_windows, segments, available, table, chunks, chunk_bins)
    packed, flipped = [], []
    for c in range(chunks):
        mine = [pieces[0][c]] + [lax.ppermute(pieces[d][c], "freq", swap[d]) for d in range(1, nodes)]
        p, f = pack_windows(me, counts, mine, chunk_bins, windows)
        packed.append(p)
        flipped.append(f)
    out = None
    scale = 1.0 / windows
    for c in range(chunks):
        block, blocks = packed[c], []
        for t in range(steps):
            blocks += [block, lax.ppermute(block, "chan", cores)]
            if t < steps - 1:
                block = lax.ppermute(block, "chan", ring)
        out = pair_products(place, flipped[c], blocks, out, bins, c, scale)
    return out


def solution(mesh):
    placed = (P("freq", "chan", None), P("freq", "chan"), P("freq"))
    return jax.shard_map(
        functools.partial(shards, mesh.shape["freq"], mesh.shape["chan"]),
        mesh=mesh,
        in_specs=placed,
        out_specs=P(None, "freq", "chan", None),
        check_vma=False,
    )
```

```python
import functools
import math

import jax
import jax.numpy as jnp
import ml_dtypes
import numpy as np
from jax import lax
from jax.experimental import pallas as pl
from jax.experimental.pallas import tpu as pltpu
from jax.sharding import PartitionSpec as P

FREQS = 128
FIRST_BIN = 64
EPSILON = 1e-06
PART_BINS = 8
CHUNK_PARTS = {4: [2, 2]}
RING = [(0, 1), (1, 1), (0, 2), (1, 2), (0, 3), (1, 3)]
DEPTH = 2
UNROLL = 4
AHEAD = 8
VMEM_LIMIT = 24 << 20
SPECTRA_VMEM = 48 << 20


def transform_table(nodes, chunk_bins, samples):
    sample_index = np.arange(samples, dtype=np.int64)[None, :]
    bin_index = (FIRST_BIN + np.arange(FREQS, dtype=np.int64))[:, None]
    angles = (bin_index * sample_index % samples).astype(np.float64) * (2.0 * math.pi / samples)
    parts = np.stack([np.cos(angles), -np.sin(angles)]).astype(np.float32).astype(ml_dtypes.bfloat16)
    return parts.reshape(2, nodes, -1, chunk_bins, samples).transpose(1, 2, 0, 3, 4).reshape(nodes, -1, samples)


def spectra_kernel(nodes, me_ref, count_ref, seg_hbm, avail_hbm, table_hbm, *refs):
    pieces = refs[:-6]
    seg_ref, avail_ref, table, table_sem, avail_sem, seg_sem = refs[-6:]
    slots = seg_ref.shape[0]
    height = table_hbm.shape[1]
    copies = [
        pltpu.make_async_copy(table_hbm.at[me_ref[0] ^ d], table.at[pl.ds(d * height, height)], table_sem.at[d])
        for d in range(nodes)
    ]
    copies.append(pltpu.make_async_copy(avail_hbm, avail_ref, avail_sem))

    def segment(w):
        return pltpu.make_async_copy(seg_hbm.at[w], seg_ref.at[w], seg_sem.at[w])

    for copy in copies:
        copy.start()
    for w in range(AHEAD):
        segment(w).start()
    for piece in pieces:
        piece[slots] = jnp.full(piece.shape[1:], count_ref[0], jnp.int32).astype(jnp.bfloat16)
    for copy in copies:
        copy.wait()

    def transform(w):
        raw = lax.dot_general(
            table[...], seg_ref[w], (((1,), (1,)), ((), ())), preferred_element_type=jnp.float32
        )
        live = jnp.where(w < count_ref[0], avail_ref[pl.ds(w, 1), :], 0).astype(jnp.float32)
        spectra = (raw * live).astype(jnp.bfloat16).astype(jnp.float32)
        energy = jnp.sum(spectra * spectra, axis=0, keepdims=True) / FREQS
        whitened = (spectra * lax.rsqrt(energy + EPSILON)).astype(jnp.bfloat16)
        low = 0
        for d in range(nodes):
            for piece in pieces[d::nodes]:
                high = low + piece.shape[1]
                piece[w] = whitened[low:high]
                low = high

    @pl.loop(0, slots, step=UNROLL)
    def _(w):
        for k in range(UNROLL):
            @pl.when(w + k + AHEAD < slots)
            def _():
                segment(w + k + AHEAD).start()
        for k in range(UNROLL):
            segment(w + k).wait()
        for k in range(UNROLL):
            transform(w + k)


def spectra_pieces(me, node_windows, segments, available, table, sizes):
    slots, chan, samples = segments.shape
    nodes = table.shape[0]
    pieces = [jax.ShapeDtypeStruct((slots + 1, size, chan), jnp.bfloat16) for size in sizes for _ in range(nodes)]
    hbm = pl.BlockSpec(memory_space=pltpu.HBM)
    smem = pl.BlockSpec(memory_space=pltpu.SMEM)
    out = pl.pallas_call(
        functools.partial(spectra_kernel, nodes),
        in_specs=[smem, smem, hbm, hbm, hbm],
        out_specs=[pl.BlockSpec(memory_space=pltpu.VMEM)] * len(pieces),
        out_shape=pieces,
        scratch_shapes=[
            pltpu.VMEM(segments.shape, jnp.bfloat16),
            pltpu.VMEM(available.shape, jnp.int32),
            pltpu.VMEM((2 * FREQS, samples), jnp.bfloat16),
            pltpu.SemaphoreType.DMA((nodes,)),
            pltpu.SemaphoreType.DMA,
            pltpu.SemaphoreType.DMA((slots,)),
        ],
        compiler_params=pltpu.CompilerParams(vmem_limit_bytes=SPECTRA_VMEM),
        cost_estimate=pl.CostEstimate(
            flops=2 * slots * chan * samples * 2 * FREQS, bytes_accessed=2 * slots * chan * samples, transcendentals=0
        ),
        name="spectra",
    )(me, node_windows, segments, available, table)
    return [list(out[g * nodes:(g + 1) * nodes]) for g in range(len(sizes))]


def pack_kernel(nodes, slots, parts, bins, windows, me_ref, *refs):
    pieces, (packed_ref, again_ref) = refs[:nodes], refs[nodes:]
    me = me_ref[0]
    chan = packed_ref.shape[2]
    out_rows, in_rows = bins * 2 * windows, slots * 2 * bins
    col = lax.broadcasted_iota(jnp.int32, (1, in_rows), 1)
    slot, half, fbin = col // (2 * bins), (col // bins) % 2, col % bins
    row = lax.broadcasted_iota(jnp.int32, (out_rows, in_rows), 0)
    counts = [piece[slots].astype(jnp.float32)[0:1, 0:1].astype(jnp.int32) for piece in pieces]
    packed = [jnp.zeros((out_rows, chan), jnp.float32) for _ in range(parts)]
    for d in range(nodes):
        start = jnp.zeros((1, 1), jnp.int32)
        for e in range(nodes):
            start = start + jnp.where((me ^ e) < (me ^ d), counts[e], 0)
        place = jnp.where(slot < counts[d], (fbin * 2 + half) * windows + start + slot, -1)
        select = jnp.where(row == place, 1.0, 0.0).astype(jnp.bfloat16)
        for p in range(parts):
            rows = pieces[d][:slots, p * 2 * bins:(p + 1) * 2 * bins].reshape(in_rows, chan)
            packed[p] += jnp.dot(select, rows, preferred_element_type=jnp.float32)
    for p in range(parts):
        block = packed[p].astype(jnp.bfloat16).reshape(bins, 2 * windows, chan)
        packed_ref[p * bins:(p + 1) * bins] = block
        again_ref[p * bins:(p + 1) * bins] = block


def pack_windows(me, pieces, held, parts, windows):
    slots, chan = pieces[0].shape[0] - 1, pieces[0].shape[2]
    nodes = len(pieces)
    bins = pieces[0].shape[1] // (2 * parts)
    whole = pl.BlockSpec(memory_space=pltpu.VMEM)
    anywhere = pl.BlockSpec(memory_space=pl.ANY)
    packed = jax.ShapeDtypeStruct((parts * bins, 2 * windows, chan), jnp.bfloat16)

    def kernel(me_ref, *refs):
        outs = refs[nodes + len(held):]
        pack_kernel(nodes, slots, parts, bins, windows, me_ref, *refs[:nodes], *outs[:2])

    result = pl.pallas_call(
        kernel,
        in_specs=[pl.BlockSpec(memory_space=pltpu.SMEM)] + [whole] * nodes + [anywhere] * len(held),
        out_specs=[whole] * 2 + [anywhere] * len(held),
        out_shape=[packed] * 2 + [jax.ShapeDtypeStruct(array.shape, array.dtype) for array in held],
        input_output_aliases={1 + nodes + k: 2 + k for k in range(len(held))},
        compiler_params=pltpu.CompilerParams(vmem_limit_bytes=VMEM_LIMIT),
        cost_estimate=pl.CostEstimate(flops=1 << 10, bytes_accessed=1 << 10, transcendentals=0),
        name="pack",
    )(me, *pieces, *held)
    return result[0], result[1], list(result[2:])


def conjugate_rows(block):
    depth, chan = block.shape
    i = lax.broadcasted_iota(jnp.int32, (depth, depth), 0)
    j = lax.broadcasted_iota(jnp.int32, (depth, depth), 1)
    half = depth // 2
    swap = jnp.where(i == j + half, 1.0, jnp.where(j == i + half, -1.0, 0.0)).astype(jnp.bfloat16)
    rows = jnp.transpose(block, (1, 0))
    return rows, jnp.dot(rows, swap, preferred_element_type=jnp.float32).astype(jnp.bfloat16)


def pairs_body(first, scale, place_ref, ours_ref, theirs_ref, *refs):
    out_ref, rows_ref = refs if first else refs[::-1]
    core = place_ref[0] % 2
    count, _, chan = ours_ref.shape
    for b in range(count):
        if first:
            rows_ref[b, :chan], rows_ref[b, chan:] = conjugate_rows(ours_ref[b])
        ours, theirs = ours_ref[b], theirs_ref[b]
        both = jnp.concatenate(
            [jnp.where(core == 0, ours, theirs), jnp.where(core == 0, theirs, ours)], axis=1
        )
        product = jnp.dot(rows_ref[b], both, preferred_element_type=jnp.float32) * scale
        product = product.astype(jnp.bfloat16)
        out_ref[0, b] = product[:chan]
        out_ref[1, b] = product[chan:]


def pair_products(place, ours, theirs, rows, out, held, bins, groups, first_bin, t, scale):
    chunk_bins, depth, chan = ours.shape
    steps = groups // 2
    per_step = math.gcd(math.gcd(chunk_bins, first_bin), 4)
    block = pl.BlockSpec((per_step, depth, chan), lambda i, p: (i, 0, 0))
    rows_spec = pl.BlockSpec((per_step, 2 * chan, depth), lambda i, p: (i, 0, 0))
    anywhere = pl.BlockSpec(memory_space=pl.ANY)
    first = rows is None
    operands, specs = [place, ours, theirs], [block, block]
    if not first:
        operands.append(rows)
        specs.append(rows_spec)
    out_spec = pl.BlockSpec(
        (2, per_step, chan, 2 * chan),
        lambda i, p: (0, first_bin // per_step + i, 0, lax.rem(p[0] // 2 - t + steps, steps)),
    )
    out_specs, out_shape = [], []
    aliases = {}
    if out is not None:
        aliases[len(operands)] = 0
        operands.append(out)
        specs.append(anywhere)
    out_specs.append(out_spec)
    out_shape.append(jax.ShapeDtypeStruct((2, bins, chan, groups * chan), jnp.bfloat16))
    if first:
        out_specs.append(rows_spec)
        out_shape.append(jax.ShapeDtypeStruct((chunk_bins, 2 * chan, depth), jnp.bfloat16))
    for array in held:
        aliases[len(operands)] = len(out_specs)
        operands.append(array)
        specs.append(anywhere)
        out_specs.append(anywhere)
        out_shape.append(jax.ShapeDtypeStruct(array.shape, array.dtype))

    def kernel(place_ref, *refs):
        ins, outs = refs[:len(specs)], refs[len(specs):]
        inner = ins[:2] + (outs[:2] if first else (ins[2], outs[0]))
        pairs_body(first, scale, place_ref, *inner)

    result = pl.pallas_call(
        kernel,
        grid_spec=pltpu.PrefetchScalarGridSpec(
            num_scalar_prefetch=1, grid=(chunk_bins // per_step,), in_specs=specs, out_specs=out_specs
        ),
        out_shape=out_shape,
        input_output_aliases=aliases,
        compiler_params=pltpu.CompilerParams(vmem_limit_bytes=VMEM_LIMIT),
        cost_estimate=pl.CostEstimate(flops=1 << 10, bytes_accessed=1 << 10, transcendentals=0),
        name="pairs",
    )(*operands)
    rows = result[1] if first else rows
    return result[0], rows, result[len(result) - len(held):]


def shards(nodes, groups, segments, available, node_windows):
    slots, chan, samples = segments.shape
    bins = FREQS // nodes
    part_bins = math.gcd(bins, PART_BINS)
    parts = CHUNK_PARTS.get(bins // part_bins, [1] * (bins // part_bins))
    starts = [sum(parts[:c]) * part_bins for c in range(len(parts))]
    chunks = len(parts)
    windows = slots * nodes * 5 // 8
    steps = groups // 2
    me = lax.axis_index("freq").astype(jnp.int32).reshape(1)
    place = lax.axis_index("chan").astype(jnp.int32).reshape(1)
    swap = [[(f, f ^ d) for f in range(nodes)] for d in range(nodes)]
    ring = [(i, (i + 2) % groups) for i in range(groups)]
    cores = [(i, i ^ 1) for i in range(groups)]

    table = jnp.asarray(transform_table(nodes, part_bins, samples))
    pieces = spectra_pieces(
        me, node_windows, segments, available, table, [2 * part_bins * count for count in parts]
    )
    ours, theirs, rows, travelling = {}, {}, {}, {}
    out = None
    scale = 1.0 / windows

    def meet(c, t):
        theirs[c, t] = lax.ppermute(ours[c, t], "chan", cores)

    def send(c, t):
        travelling[c, t] = lax.ppermute(travelling[c, t - 1], "chan", ring)

    def multiply(c, t, held=()):
        nonlocal out
        out, rows[c], kept = pair_products(
            place, ours[c, t], theirs[c, t], rows.get(c), out, list(held), bins, groups, starts[c], t, scale
        )
        return list(kept)

    for c in range(chunks):
        exchanged = [pieces[c][0]] + [lax.ppermute(pieces[c][d], "freq", swap[d]) for d in range(1, nodes)]
        held = pieces[c + 1][-1:] if c + 1 < chunks else []
        travelling[c, 0], ours[c, 0], kept = pack_windows(me, exchanged, held, parts[c], windows)
        if held:
            pieces[c + 1][-1:] = kept

    order = RING if chunks == 2 and steps == 4 else [(c, t) for t in range(1, steps) for c in range(chunks)]
    sent = 0

    def launch(done):
        nonlocal sent
        while sent < len(order) and sent < done + DEPTH:
            c, t = order[sent]
            if t > 1 and order.index((c, t - 1)) >= done:
                return
            send(c, t)
            sent += 1

    launch(0)
    meet(0, 0)
    multiply(0, 0)
    ready = []
    if chunks > 1:
        meet(1, 0)
        ready.append((1, 0))
    for k, now in enumerate(order):
        if ready:
            (travelling[now],) = multiply(*ready.pop(0), [travelling[now]])
        ours[now] = travelling[now]
        launch(k + 1)
        meet(*now)
        ready.append(now)
        if now[1] == 1 and now[0] not in rows and (now[0], 0) not in ready:
            meet(now[0], 0)
            multiply(now[0], 0)
    while ready:
        multiply(*ready.pop(0))
    return out


def solution(mesh):
    placed = (P("freq", "chan", None), P("freq", "chan"), P("freq"))
    return jax.shard_map(
        functools.partial(shards, mesh.shape["freq"], mesh.shape["chan"]),
        mesh=mesh,
        in_specs=placed,
        out_specs=P(None, "freq", "chan", None),
        check_vma=False,
    )
```

```python
import functools
import math

import jax
import jax.numpy as jnp
import ml_dtypes
import numpy as np
from jax import lax
from jax.experimental import pallas as pl
from jax.experimental.pallas import tpu as pltpu
from jax.sharding import PartitionSpec as P

FREQS = 128
FIRST_BIN = 64
EPSILON = 1e-06
PART_BINS = 8
CHUNK_PARTS = {4: [2, 2]}
RING = [(0, 1), (1, 1), (0, 2), (1, 2), (0, 3), (1, 3)]
DEPTH = 2
UNROLL = 4
AHEAD = 8
VMEM_LIMIT = 24 << 20
SPECTRA_VMEM = 48 << 20


def transform_table(nodes, chunk_bins, samples):
    sample_index = np.arange(samples, dtype=np.int64)[None, :]
    bin_index = (FIRST_BIN + np.arange(FREQS, dtype=np.int64))[:, None]
    angles = (bin_index * sample_index % samples).astype(np.float64) * (2.0 * math.pi / samples)
    parts = np.stack([np.cos(angles), -np.sin(angles)]).astype(np.float32).astype(ml_dtypes.bfloat16)
    return parts.reshape(2, nodes, -1, chunk_bins, samples).transpose(1, 2, 0, 3, 4).reshape(nodes, -1, samples)


def spectra_kernel(nodes, me_ref, count_ref, seg_hbm, avail_hbm, table_hbm, *refs):
    pieces = refs[:-6]
    seg_ref, avail_ref, table, table_sem, avail_sem, seg_sem = refs[-6:]
    slots = seg_ref.shape[0]
    height = table_hbm.shape[1]
    copies = [
        pltpu.make_async_copy(table_hbm.at[me_ref[0] ^ d], table.at[pl.ds(d * height, height)], table_sem.at[d])
        for d in range(nodes)
    ]
    copies.append(pltpu.make_async_copy(avail_hbm, avail_ref, avail_sem))

    def segment(w):
        return pltpu.make_async_copy(seg_hbm.at[w], seg_ref.at[w], seg_sem.at[w])

    for copy in copies:
        copy.start()
    for w in range(AHEAD):
        segment(w).start()
    for piece in pieces:
        piece[slots] = jnp.full(piece.shape[1:], count_ref[0], jnp.int32).astype(jnp.bfloat16)
    for copy in copies:
        copy.wait()

    def transform(w):
        raw = lax.dot_general(
            table[...], seg_ref[w], (((1,), (1,)), ((), ())), preferred_element_type=jnp.float32
        )
        live = jnp.where(w < count_ref[0], avail_ref[pl.ds(w, 1), :], 0).astype(jnp.float32)
        spectra = (raw * live).astype(jnp.bfloat16).astype(jnp.float32)
        energy = jnp.sum(spectra * spectra, axis=0, keepdims=True) / FREQS
        whitened = (spectra * lax.rsqrt(energy + EPSILON)).astype(jnp.bfloat16)
        low = 0
        for d in range(nodes):
            for piece in pieces[d::nodes]:
                high = low + piece.shape[1]
                piece[w] = whitened[low:high]
                low = high

    @pl.loop(0, slots, step=UNROLL)
    def _(w):
        for k in range(UNROLL):
            @pl.when(w + k + AHEAD < slots)
            def _():
                segment(w + k + AHEAD).start()
        for k in range(UNROLL):
            segment(w + k).wait()
        for k in range(UNROLL):
            transform(w + k)


def spectra_pieces(me, node_windows, segments, available, table, sizes):
    slots, chan, samples = segments.shape
    nodes = table.shape[0]
    pieces = [jax.ShapeDtypeStruct((slots + 1, size, chan), jnp.bfloat16) for size in sizes for _ in range(nodes)]
    hbm = pl.BlockSpec(memory_space=pltpu.HBM)
    smem = pl.BlockSpec(memory_space=pltpu.SMEM)
    out = pl.pallas_call(
        functools.partial(spectra_kernel, nodes),
        in_specs=[smem, smem, hbm, hbm, hbm],
        out_specs=[pl.BlockSpec(memory_space=pltpu.VMEM)] * len(pieces),
        out_shape=pieces,
        scratch_shapes=[
            pltpu.VMEM(segments.shape, jnp.bfloat16),
            pltpu.VMEM(available.shape, jnp.int32),
            pltpu.VMEM((2 * FREQS, samples), jnp.bfloat16),
            pltpu.SemaphoreType.DMA((nodes,)),
            pltpu.SemaphoreType.DMA,
            pltpu.SemaphoreType.DMA((slots,)),
        ],
        compiler_params=pltpu.CompilerParams(vmem_limit_bytes=SPECTRA_VMEM),
        cost_estimate=pl.CostEstimate(
            flops=2 * slots * chan * samples * 2 * FREQS, bytes_accessed=2 * slots * chan * samples, transcendentals=0
        ),
        name="spectra",
    )(me, node_windows, segments, available, table)
    return [list(out[g * nodes:(g + 1) * nodes]) for g in range(len(sizes))]


def pack_kernel(nodes, slots, parts, bins, windows, me_ref, *refs):
    pieces, (packed_ref, again_ref) = refs[:nodes], refs[nodes:]
    me = me_ref[0]
    chan = packed_ref.shape[2]
    out_rows, in_rows = bins * 2 * windows, slots * 2 * bins
    col = lax.broadcasted_iota(jnp.int32, (1, in_rows), 1)
    slot, half, fbin = col // (2 * bins), (col // bins) % 2, col % bins
    row = lax.broadcasted_iota(jnp.int32, (out_rows, in_rows), 0)
    counts = [piece[slots].astype(jnp.float32)[0:1, 0:1].astype(jnp.int32) for piece in pieces]
    packed = [jnp.zeros((out_rows, chan), jnp.float32) for _ in range(parts)]
    for d in range(nodes):
        start = jnp.zeros((1, 1), jnp.int32)
        for e in range(nodes):
            start = start + jnp.where((me ^ e) < (me ^ d), counts[e], 0)
        place = jnp.where(slot < counts[d], (fbin * 2 + half) * windows + start + slot, -1)
        select = jnp.where(row == place, 1.0, 0.0).astype(jnp.bfloat16)
        for p in range(parts):
            rows = pieces[d][:slots, p * 2 * bins:(p + 1) * 2 * bins].reshape(in_rows, chan)
            packed[p] += jnp.dot(select, rows, preferred_element_type=jnp.float32)
    for p in range(parts):
        block = packed[p].astype(jnp.bfloat16).reshape(bins, 2 * windows, chan)
        packed_ref[p * bins:(p + 1) * bins] = block
        again_ref[p * bins:(p + 1) * bins] = block


def pack_windows(me, pieces, held, parts, windows):
    slots, chan = pieces[0].shape[0] - 1, pieces[0].shape[2]
    nodes = len(pieces)
    bins = pieces[0].shape[1] // (2 * parts)
    whole = pl.BlockSpec(memory_space=pltpu.VMEM)
    anywhere = pl.BlockSpec(memory_space=pl.ANY)
    packed = jax.ShapeDtypeStruct((parts * bins, 2 * windows, chan), jnp.bfloat16)

    def kernel(me_ref, *refs):
        outs = refs[nodes + len(held):]
        pack_kernel(nodes, slots, parts, bins, windows, me_ref, *refs[:nodes], *outs[:2])

    result = pl.pallas_call(
        kernel,
        in_specs=[pl.BlockSpec(memory_space=pltpu.SMEM)] + [whole] * nodes + [anywhere] * len(held),
        out_specs=[whole] * 2 + [anywhere] * len(held),
        out_shape=[packed] * 2 + [jax.ShapeDtypeStruct(array.shape, array.dtype) for array in held],
        input_output_aliases={1 + nodes + k: 2 + k for k in range(len(held))},
        compiler_params=pltpu.CompilerParams(vmem_limit_bytes=VMEM_LIMIT),
        cost_estimate=pl.CostEstimate(flops=1 << 10, bytes_accessed=1 << 10, transcendentals=0),
        name="pack",
    )(me, *pieces, *held)
    return result[0], result[1], list(result[2:])


def conjugate_rows(block):
    depth, chan = block.shape
    i = lax.broadcasted_iota(jnp.int32, (depth, depth), 0)
    j = lax.broadcasted_iota(jnp.int32, (depth, depth), 1)
    half = depth // 2
    swap = jnp.where(i == j + half, 1.0, jnp.where(j == i + half, -1.0, 0.0)).astype(jnp.bfloat16)
    rows = jnp.transpose(block, (1, 0))
    return rows, jnp.dot(rows, swap, preferred_element_type=jnp.float32).astype(jnp.bfloat16)


def pairs_body(first, scale, place_ref, ours_ref, theirs_ref, *refs):
    out_ref, rows_ref = refs if first else refs[::-1]
    core = place_ref[0] % 2
    count, _, chan = ours_ref.shape
    for b in range(count):
        if first:
            rows_ref[b, :chan], rows_ref[b, chan:] = conjugate_rows(ours_ref[b])
        ours, theirs = ours_ref[b], theirs_ref[b]
        both = jnp.concatenate(
            [jnp.where(core == 0, ours, theirs), jnp.where(core == 0, theirs, ours)], axis=1
        )
        product = jnp.dot(rows_ref[b], both, preferred_element_type=jnp.float32) * scale
        product = product.astype(jnp.bfloat16)
        out_ref[0, b] = product[:chan]
        out_ref[1, b] = product[chan:]


def pair_products(place, ours, theirs, rows, out, held, bins, groups, first_bin, t, scale):
    chunk_bins, depth, chan = ours.shape
    steps = groups // 2
    per_step = math.gcd(math.gcd(chunk_bins, first_bin), 4)
    block = pl.BlockSpec((per_step, depth, chan), lambda i, p: (i, 0, 0))
    rows_spec = pl.BlockSpec((per_step, 2 * chan, depth), lambda i, p: (i, 0, 0))
    anywhere = pl.BlockSpec(memory_space=pl.ANY)
    first = rows is None
    operands, specs = [place, ours, theirs], [block, block]
    if not first:
        operands.append(rows)
        specs.append(rows_spec)
    out_spec = pl.BlockSpec(
        (2, per_step, chan, 2 * chan),
        lambda i, p: (0, first_bin // per_step + i, 0, lax.rem(p[0] // 2 - t + steps, steps)),
    )
    out_specs, out_shape = [], []
    aliases = {}
    if out is not None:
        aliases[len(operands)] = 0
        operands.append(out)
        specs.append(anywhere)
    out_specs.append(out_spec)
    out_shape.append(jax.ShapeDtypeStruct((2, bins, chan, groups * chan), jnp.bfloat16))
    if first:
        out_specs.append(rows_spec)
        out_shape.append(jax.ShapeDtypeStruct((chunk_bins, 2 * chan, depth), jnp.bfloat16))
    for array in held:
        aliases[len(operands)] = len(out_specs)
        operands.append(array)
        specs.append(anywhere)
        out_specs.append(anywhere)
        out_shape.append(jax.ShapeDtypeStruct(array.shape, array.dtype))

    def kernel(place_ref, *refs):
        ins, outs = refs[:len(specs)], refs[len(specs):]
        inner = ins[:2] + (outs[:2] if first else (ins[2], outs[0]))
        pairs_body(first, scale, place_ref, *inner)

    result = pl.pallas_call(
        kernel,
        grid_spec=pltpu.PrefetchScalarGridSpec(
            num_scalar_prefetch=1, grid=(chunk_bins // per_step,), in_specs=specs, out_specs=out_specs
        ),
        out_shape=out_shape,
        input_output_aliases=aliases,
        compiler_params=pltpu.CompilerParams(vmem_limit_bytes=VMEM_LIMIT),
        cost_estimate=pl.CostEstimate(flops=1 << 10, bytes_accessed=1 << 10, transcendentals=0),
        name="pairs",
    )(*operands)
    rows = result[1] if first else rows
    return result[0], rows, result[len(result) - len(held):]


def shards(nodes, groups, segments, available, node_windows):
    slots, chan, samples = segments.shape
    bins = FREQS // nodes
    part_bins = math.gcd(bins, PART_BINS)
    parts = CHUNK_PARTS.get(bins // part_bins, [1] * (bins // part_bins))
    starts = [sum(parts[:c]) * part_bins for c in range(len(parts))]
    chunks = len(parts)
    windows = slots * nodes * 5 // 8
    steps = groups // 2
    me = lax.axis_index("freq").astype(jnp.int32).reshape(1)
    place = lax.axis_index("chan").astype(jnp.int32).reshape(1)
    swap = [[(f, f ^ d) for f in range(nodes)] for d in range(nodes)]
    ring = [(i, (i + 2) % groups) for i in range(groups)]
    cores = [(i, i ^ 1) for i in range(groups)]

    table = jnp.asarray(transform_table(nodes, part_bins, samples))
    pieces = spectra_pieces(
        me, node_windows, segments, available, table, [2 * part_bins * count for count in parts]
    )
    ours, theirs, rows, travelling = {}, {}, {}, {}
    out = None
    scale = 1.0 / windows

    def meet(c, t):
        theirs[c, t] = lax.ppermute(ours[c, t], "chan", cores)

    def send(c, t):
        travelling[c, t] = lax.ppermute(travelling[c, t - 1], "chan", ring)

    def multiply(c, t, held=()):
        nonlocal out
        out, rows[c], kept = pair_products(
            place, ours[c, t], theirs[c, t], rows.get(c), out, list(held), bins, groups, starts[c], t, scale
        )
        return list(kept)

    for c in range(chunks):
        exchanged = [pieces[c][0]] + [lax.ppermute(pieces[c][d], "freq", swap[d]) for d in range(1, nodes)]
        held = pieces[c + 1][-1:] if c + 1 < chunks else []
        travelling[c, 0], ours[c, 0], kept = pack_windows(me, exchanged, held, parts[c], windows)
        if held:
            pieces[c + 1][-1:] = kept

    order = RING if chunks == 2 and steps == 4 else [(c, t) for t in range(1, steps) for c in range(chunks)]
    sent = 0

    def launch(done):
        nonlocal sent
        while sent < len(order) and sent < done + DEPTH:
            c, t = order[sent]
            if t > 1 and order.index((c, t - 1)) >= done:
                return
            send(c, t)
            sent += 1

    launch(0)
    meet(0, 0)
    multiply(0, 0)
    ready = []
    if chunks > 1:
        meet(1, 0)
        ready.append((1, 0))
    for k, now in enumerate(order):
        if ready and k + 1 < len(order):
            (travelling[now],) = multiply(*ready.pop(0), [travelling[now]])
        ours[now] = travelling[now]
        launch(k + 1)
        meet(*now)
        ready.append(now)
        if now[1] == 1 and now[0] not in rows and (now[0], 0) not in ready:
            meet(now[0], 0)
            multiply(now[0], 0)
    while ready:
        multiply(*ready.pop(0))
    return out


def solution(mesh):
    placed = (P("freq", "chan", None), P("freq", "chan"), P("freq"))
    return jax.shard_map(
        functools.partial(shards, mesh.shape["freq"], mesh.shape["chan"]),
        mesh=mesh,
        in_specs=placed,
        out_specs=P(None, "freq", "chan", None),
        check_vma=False,
    )
```

```python
import functools
import math

import jax
import jax.numpy as jnp
import ml_dtypes
import numpy as np
from jax import lax
from jax.experimental import pallas as pl
from jax.experimental.pallas import tpu as pltpu
from jax.sharding import PartitionSpec as P

FREQS = 128
FIRST_BIN = 64
EPSILON = 1e-06
PART_BINS = 8
CHUNK_PARTS = {4: [2, 2]}
RING = [(0, 1), (1, 1), (0, 2), (1, 2), (0, 3), (1, 3)]
DEPTH = 2
UNROLL = 4
AHEAD = 8
VMEM_LIMIT = 24 << 20
SPECTRA_VMEM = 48 << 20


def transform_table(nodes, chunk_bins, samples):
    sample_index = np.arange(samples, dtype=np.int64)[None, :]
    bin_index = (FIRST_BIN + np.arange(FREQS, dtype=np.int64))[:, None]
    angles = (bin_index * sample_index % samples).astype(np.float64) * (2.0 * math.pi / samples)
    parts = np.stack([np.cos(angles), -np.sin(angles)]).astype(np.float32).astype(ml_dtypes.bfloat16)
    return parts.reshape(2, nodes, -1, chunk_bins, samples).transpose(1, 2, 0, 3, 4).reshape(nodes, -1, samples)


def spectra_kernel(nodes, me_ref, count_ref, seg_hbm, avail_hbm, table_hbm, *refs):
    pieces = refs[:-6]
    seg_ref, avail_ref, table, table_sem, avail_sem, seg_sem = refs[-6:]
    slots = seg_ref.shape[0]
    height = table_hbm.shape[1]
    copies = [
        pltpu.make_async_copy(table_hbm.at[me_ref[0] ^ d], table.at[pl.ds(d * height, height)], table_sem.at[d])
        for d in range(nodes)
    ]
    copies.append(pltpu.make_async_copy(avail_hbm, avail_ref, avail_sem))

    def segment(w):
        return pltpu.make_async_copy(seg_hbm.at[w], seg_ref.at[w], seg_sem.at[w])

    for copy in copies:
        copy.start()
    for w in range(AHEAD):
        segment(w).start()
    for piece in pieces:
        piece[slots] = jnp.full(piece.shape[1:], count_ref[0], jnp.int32).astype(jnp.bfloat16)
    for copy in copies:
        copy.wait()

    def transform(w):
        raw = lax.dot_general(
            table[...], seg_ref[w], (((1,), (1,)), ((), ())), preferred_element_type=jnp.float32
        )
        live = jnp.where(w < count_ref[0], avail_ref[pl.ds(w, 1), :], 0).astype(jnp.float32)
        spectra = (raw * live).astype(jnp.bfloat16).astype(jnp.float32)
        energy = jnp.sum(spectra * spectra, axis=0, keepdims=True) / FREQS
        whitened = (spectra * lax.rsqrt(energy + EPSILON)).astype(jnp.bfloat16)
        low = 0
        for d in range(nodes):
            for piece in pieces[d::nodes]:
                high = low + piece.shape[1]
                piece[w] = whitened[low:high]
                low = high

    @pl.loop(0, slots, step=UNROLL)
    def _(w):
        for k in range(UNROLL):
            @pl.when(w + k + AHEAD < slots)
            def _():
                segment(w + k + AHEAD).start()
        for k in range(UNROLL):
            segment(w + k).wait()
        for k in range(UNROLL):
            transform(w + k)


def spectra_pieces(me, node_windows, segments, available, table, sizes):
    slots, chan, samples = segments.shape
    nodes = table.shape[0]
    pieces = [jax.ShapeDtypeStruct((slots + 1, size, chan), jnp.bfloat16) for size in sizes for _ in range(nodes)]
    hbm = pl.BlockSpec(memory_space=pltpu.HBM)
    smem = pl.BlockSpec(memory_space=pltpu.SMEM)
    out = pl.pallas_call(
        functools.partial(spectra_kernel, nodes),
        in_specs=[smem, smem, hbm, hbm, hbm],
        out_specs=[pl.BlockSpec(memory_space=pltpu.VMEM)] * len(pieces),
        out_shape=pieces,
        scratch_shapes=[
            pltpu.VMEM(segments.shape, jnp.bfloat16),
            pltpu.VMEM(available.shape, jnp.int32),
            pltpu.VMEM((2 * FREQS, samples), jnp.bfloat16),
            pltpu.SemaphoreType.DMA((nodes,)),
            pltpu.SemaphoreType.DMA,
            pltpu.SemaphoreType.DMA((slots,)),
        ],
        compiler_params=pltpu.CompilerParams(vmem_limit_bytes=SPECTRA_VMEM),
        cost_estimate=pl.CostEstimate(
            flops=2 * slots * chan * samples * 2 * FREQS, bytes_accessed=2 * slots * chan * samples, transcendentals=0
        ),
        name="spectra",
    )(me, node_windows, segments, available, table)
    return [list(out[g * nodes:(g + 1) * nodes]) for g in range(len(sizes))]


def pack_kernel(nodes, slots, parts, bins, windows, me_ref, *refs):
    pieces, (packed_ref, again_ref) = refs[:nodes], refs[nodes:]
    me = me_ref[0]
    chan = packed_ref.shape[2]
    out_rows, in_rows = bins * 2 * windows, slots * 2 * bins
    col = lax.broadcasted_iota(jnp.int32, (1, in_rows), 1)
    slot, half, fbin = col // (2 * bins), (col // bins) % 2, col % bins
    row = lax.broadcasted_iota(jnp.int32, (out_rows, in_rows), 0)
    counts = [piece[slots].astype(jnp.float32)[0:1, 0:1].astype(jnp.int32) for piece in pieces]
    packed = [jnp.zeros((out_rows, chan), jnp.float32) for _ in range(parts)]
    for d in range(nodes):
        start = jnp.zeros((1, 1), jnp.int32)
        for e in range(nodes):
            start = start + jnp.where((me ^ e) < (me ^ d), counts[e], 0)
        place = jnp.where(slot < counts[d], (fbin * 2 + half) * windows + start + slot, -1)
        select = jnp.where(row == place, 1.0, 0.0).astype(jnp.bfloat16)
        for p in range(parts):
            rows = pieces[d][:slots, p * 2 * bins:(p + 1) * 2 * bins].reshape(in_rows, chan)
            packed[p] += jnp.dot(select, rows, preferred_element_type=jnp.float32)
    for p in range(parts):
        block = packed[p].astype(jnp.bfloat16).reshape(bins, 2 * windows, chan)
        packed_ref[p * bins:(p + 1) * bins] = block
        again_ref[p * bins:(p + 1) * bins] = block


def pack_windows(me, pieces, held, parts, windows):
    slots, chan = pieces[0].shape[0] - 1, pieces[0].shape[2]
    nodes = len(pieces)
    bins = pieces[0].shape[1] // (2 * parts)
    whole = pl.BlockSpec(memory_space=pltpu.VMEM)
    anywhere = pl.BlockSpec(memory_space=pl.ANY)
    packed = jax.ShapeDtypeStruct((parts * bins, 2 * windows, chan), jnp.bfloat16)

    def kernel(me_ref, *refs):
        outs = refs[nodes + len(held):]
        pack_kernel(nodes, slots, parts, bins, windows, me_ref, *refs[:nodes], *outs[:2])

    result = pl.pallas_call(
        kernel,
        in_specs=[pl.BlockSpec(memory_space=pltpu.SMEM)] + [whole] * nodes + [anywhere] * len(held),
        out_specs=[whole] * 2 + [anywhere] * len(held),
        out_shape=[packed] * 2 + [jax.ShapeDtypeStruct(array.shape, array.dtype) for array in held],
        input_output_aliases={1 + nodes + k: 2 + k for k in range(len(held))},
        compiler_params=pltpu.CompilerParams(vmem_limit_bytes=VMEM_LIMIT),
        cost_estimate=pl.CostEstimate(flops=1 << 10, bytes_accessed=1 << 10, transcendentals=0),
        name="pack",
    )(me, *pieces, *held)
    return result[0], result[1], list(result[2:])


def conjugate_rows(block):
    depth, chan = block.shape
    i = lax.broadcasted_iota(jnp.int32, (depth, depth), 0)
    j = lax.broadcasted_iota(jnp.int32, (depth, depth), 1)
    half = depth // 2
    swap = jnp.where(i == j + half, 1.0, jnp.where(j == i + half, -1.0, 0.0)).astype(jnp.bfloat16)
    rows = jnp.transpose(block, (1, 0))
    return rows, jnp.dot(rows, swap, preferred_element_type=jnp.float32).astype(jnp.bfloat16)


def pairs_body(first, scale, place_ref, ours_ref, theirs_ref, *refs):
    out_ref, rows_ref = refs if first else refs[::-1]
    core = place_ref[0] % 2
    count, _, chan = ours_ref.shape
    for b in range(count):
        if first:
            rows_ref[b, :chan], rows_ref[b, chan:] = conjugate_rows(ours_ref[b])
        ours, theirs = ours_ref[b], theirs_ref[b]
        both = jnp.concatenate(
            [jnp.where(core == 0, ours, theirs), jnp.where(core == 0, theirs, ours)], axis=1
        )
        product = jnp.dot(rows_ref[b], both, preferred_element_type=jnp.float32) * scale
        product = product.astype(jnp.bfloat16)
        out_ref[0, b] = product[:chan]
        out_ref[1, b] = product[chan:]


def pair_products(place, ours, theirs, rows, out, held, bins, groups, first_bin, t, scale):
    chunk_bins, depth, chan = ours.shape
    steps = groups // 2
    per_step = math.gcd(math.gcd(chunk_bins, first_bin), 4)
    block = pl.BlockSpec((per_step, depth, chan), lambda i, p: (i, 0, 0))
    rows_spec = pl.BlockSpec((per_step, 2 * chan, depth), lambda i, p: (i, 0, 0))
    anywhere = pl.BlockSpec(memory_space=pl.ANY)
    first = rows is None
    operands, specs = [place, ours, theirs], [block, block]
    if not first:
        operands.append(rows)
        specs.append(rows_spec)
    out_spec = pl.BlockSpec(
        (2, per_step, chan, 2 * chan),
        lambda i, p: (0, first_bin // per_step + i, 0, lax.rem(p[0] // 2 - t + steps, steps)),
    )
    out_specs, out_shape = [], []
    aliases = {}
    if out is not None:
        aliases[len(operands)] = 0
        operands.append(out)
        specs.append(anywhere)
    out_specs.append(out_spec)
    out_shape.append(jax.ShapeDtypeStruct((2, bins, chan, groups * chan), jnp.bfloat16))
    if first:
        out_specs.append(rows_spec)
        out_shape.append(jax.ShapeDtypeStruct((chunk_bins, 2 * chan, depth), jnp.bfloat16))
    for array in held:
        aliases[len(operands)] = len(out_specs)
        operands.append(array)
        specs.append(anywhere)
        out_specs.append(anywhere)
        out_shape.append(jax.ShapeDtypeStruct(array.shape, array.dtype))

    def kernel(place_ref, *refs):
        ins, outs = refs[:len(specs)], refs[len(specs):]
        inner = ins[:2] + (outs[:2] if first else (ins[2], outs[0]))
        pairs_body(first, scale, place_ref, *inner)

    result = pl.pallas_call(
        kernel,
        grid_spec=pltpu.PrefetchScalarGridSpec(
            num_scalar_prefetch=1, grid=(chunk_bins // per_step,), in_specs=specs, out_specs=out_specs
        ),
        out_shape=out_shape,
        input_output_aliases=aliases,
        compiler_params=pltpu.CompilerParams(vmem_limit_bytes=VMEM_LIMIT),
        cost_estimate=pl.CostEstimate(flops=1 << 10, bytes_accessed=1 << 10, transcendentals=0),
        name="pairs",
    )(*operands)
    rows = result[1] if first else rows
    return result[0], rows, result[len(result) - len(held):]


def shards(nodes, groups, segments, available, node_windows):
    slots, chan, samples = segments.shape
    bins = FREQS // nodes
    part_bins = math.gcd(bins, PART_BINS)
    parts = CHUNK_PARTS.get(bins // part_bins, [1] * (bins // part_bins))
    starts = [sum(parts[:c]) * part_bins for c in range(len(parts))]
    chunks = len(parts)
    windows = slots * nodes * 5 // 8
    steps = groups // 2
    me = lax.axis_index("freq").astype(jnp.int32).reshape(1)
    place = lax.axis_index("chan").astype(jnp.int32).reshape(1)
    swap = [[(f, f ^ d) for f in range(nodes)] for d in range(nodes)]
    ring = [(i, (i + 2) % groups) for i in range(groups)]
    cores = [(i, i ^ 1) for i in range(groups)]

    table = jnp.asarray(transform_table(nodes, part_bins, samples))
    pieces = spectra_pieces(
        me, node_windows, segments, available, table, [2 * part_bins * count for count in parts]
    )
    ours, theirs, rows, travelling = {}, {}, {}, {}
    out = None
    scale = 1.0 / windows

    def meet(c, t):
        theirs[c, t] = lax.ppermute(ours[c, t], "chan", cores)

    def send(c, t):
        travelling[c, t] = lax.ppermute(travelling[c, t - 1], "chan", ring)

    def multiply(c, t, held=()):
        nonlocal out
        out, rows[c], kept = pair_products(
            place, ours[c, t], theirs[c, t], rows.get(c), out, list(held), bins, groups, starts[c], t, scale
        )
        return list(kept)

    for c in reversed(range(chunks)):
        exchanged = [pieces[c][0]] + [lax.ppermute(pieces[c][d], "freq", swap[d]) for d in range(1, nodes)]
        held = []
        travelling[c, 0], ours[c, 0], kept = pack_windows(me, exchanged, held, parts[c], windows)
        if held:
            pieces[c + 1][-1:] = kept

    order = RING if chunks == 2 and steps == 4 else [(c, t) for t in range(1, steps) for c in range(chunks)]
    sent = 0

    def launch(done):
        nonlocal sent
        while sent < len(order) and sent < done + DEPTH:
            c, t = order[sent]
            if t > 1 and order.index((c, t - 1)) >= done:
                return
            send(c, t)
            sent += 1

    launch(0)
    meet(0, 0)
    multiply(0, 0)
    ready = []
    if chunks > 1:
        meet(1, 0)
        ready.append((1, 0))
    for k, now in enumerate(order):
        if ready and k + 1 < len(order):
            (travelling[now],) = multiply(*ready.pop(0), [travelling[now]])
        ours[now] = travelling[now]
        launch(k + 1)
        meet(*now)
        ready.append(now)
        if now[1] == 1 and now[0] not in rows and (now[0], 0) not in ready:
            meet(now[0], 0)
            multiply(now[0], 0)
    while ready:
        multiply(*ready.pop(0))
    return out


def solution(mesh):
    placed = (P("freq", "chan", None), P("freq", "chan"), P("freq"))
    return jax.shard_map(
        functools.partial(shards, mesh.shape["freq"], mesh.shape["chan"]),
        mesh=mesh,
        in_specs=placed,
        out_specs=P(None, "freq", "chan", None),
        check_vma=False,
    )
```

```python
import functools
import math

import jax
import jax.numpy as jnp
import ml_dtypes
import numpy as np
from jax import lax
from jax.experimental import pallas as pl
from jax.experimental.pallas import tpu as pltpu
from jax.sharding import PartitionSpec as P

FREQS = 128
FIRST_BIN = 64
EPSILON = 1e-06
PART_BINS = 8
CHUNK_PARTS = {4: [2, 2]}
RING = [(0, 1), (1, 1), (0, 2), (1, 2), (0, 3), (1, 3)]
DEPTH = 2
UNROLL = 4
AHEAD = 8
VMEM_LIMIT = 24 << 20
SPECTRA_VMEM = 48 << 20


def transform_table(nodes, chunk_bins, samples):
    sample_index = np.arange(samples, dtype=np.int64)[None, :]
    bin_index = (FIRST_BIN + np.arange(FREQS, dtype=np.int64))[:, None]
    angles = (bin_index * sample_index % samples).astype(np.float64) * (2.0 * math.pi / samples)
    parts = np.stack([np.cos(angles), -np.sin(angles)]).astype(np.float32).astype(ml_dtypes.bfloat16)
    return parts.reshape(2, nodes, -1, chunk_bins, samples).transpose(1, 2, 0, 3, 4).reshape(nodes, -1, samples)


def spectra_kernel(nodes, me_ref, count_ref, seg_hbm, avail_hbm, table_hbm, *refs):
    pieces = refs[:-6]
    seg_ref, avail_ref, table, table_sem, avail_sem, seg_sem = refs[-6:]
    slots = seg_ref.shape[0]
    height = table_hbm.shape[1]
    copies = [
        pltpu.make_async_copy(table_hbm.at[me_ref[0] ^ d], table.at[pl.ds(d * height, height)], table_sem.at[d])
        for d in range(nodes)
    ]
    copies.append(pltpu.make_async_copy(avail_hbm, avail_ref, avail_sem))

    def segment(w):
        return pltpu.make_async_copy(seg_hbm.at[w], seg_ref.at[w], seg_sem.at[w])

    for copy in copies:
        copy.start()
    for w in range(AHEAD):
        segment(w).start()
    for piece in pieces:
        piece[slots] = jnp.full(piece.shape[1:], count_ref[0], jnp.int32).astype(jnp.bfloat16)
    for copy in copies:
        copy.wait()

    def transform(w):
        raw = lax.dot_general(
            table[...], seg_ref[w], (((1,), (1,)), ((), ())), preferred_element_type=jnp.float32
        )
        live = jnp.where(w < count_ref[0], avail_ref[pl.ds(w, 1), :], 0).astype(jnp.float32)
        spectra = (raw * live).astype(jnp.bfloat16).astype(jnp.float32)
        energy = jnp.sum(spectra * spectra, axis=0, keepdims=True) / FREQS
        whitened = (spectra * lax.rsqrt(energy + EPSILON)).astype(jnp.bfloat16)
        low = 0
        for d in range(nodes):
            for piece in pieces[d::nodes]:
                high = low + piece.shape[1]
                piece[w] = whitened[low:high]
                low = high

    @pl.loop(0, slots, step=UNROLL)
    def _(w):
        for k in range(UNROLL):
            @pl.when(w + k + AHEAD < slots)
            def _():
                segment(w + k + AHEAD).start()
        for k in range(UNROLL):
            segment(w + k).wait()
        for k in range(UNROLL):
            transform(w + k)


def spectra_pieces(me, node_windows, segments, available, table, sizes):
    slots, chan, samples = segments.shape
    nodes = table.shape[0]
    pieces = [jax.ShapeDtypeStruct((slots + 1, size, chan), jnp.bfloat16) for size in sizes for _ in range(nodes)]
    hbm = pl.BlockSpec(memory_space=pltpu.HBM)
    smem = pl.BlockSpec(memory_space=pltpu.SMEM)
    out = pl.pallas_call(
        functools.partial(spectra_kernel, nodes),
        in_specs=[smem, smem, hbm, hbm, hbm],
        out_specs=[pl.BlockSpec(memory_space=pltpu.VMEM)] * len(pieces),
        out_shape=pieces,
        scratch_shapes=[
            pltpu.VMEM(segments.shape, jnp.bfloat16),
            pltpu.VMEM(available.shape, jnp.int32),
            pltpu.VMEM((2 * FREQS, samples), jnp.bfloat16),
            pltpu.SemaphoreType.DMA((nodes,)),
            pltpu.SemaphoreType.DMA,
            pltpu.SemaphoreType.DMA((slots,)),
        ],
        compiler_params=pltpu.CompilerParams(vmem_limit_bytes=SPECTRA_VMEM),
        cost_estimate=pl.CostEstimate(
            flops=2 * slots * chan * samples * 2 * FREQS, bytes_accessed=2 * slots * chan * samples, transcendentals=0
        ),
        name="spectra",
    )(me, node_windows, segments, available, table)
    return [list(out[g * nodes:(g + 1) * nodes]) for g in range(len(sizes))]


def pack_kernel(nodes, slots, parts, bins, windows, me_ref, *refs):
    pieces, (packed_ref, again_ref) = refs[:nodes], refs[nodes:]
    me = me_ref[0]
    chan = packed_ref.shape[2]
    out_rows, in_rows = bins * 2 * windows, slots * 2 * bins
    col = lax.broadcasted_iota(jnp.int32, (1, in_rows), 1)
    slot, half, fbin = col // (2 * bins), (col // bins) % 2, col % bins
    row = lax.broadcasted_iota(jnp.int32, (out_rows, in_rows), 0)
    counts = [piece[slots].astype(jnp.float32)[0:1, 0:1].astype(jnp.int32) for piece in pieces]
    packed = [jnp.zeros((out_rows, chan), jnp.float32) for _ in range(parts)]
    for d in range(nodes):
        start = jnp.zeros((1, 1), jnp.int32)
        for e in range(nodes):
            start = start + jnp.where((me ^ e) < (me ^ d), counts[e], 0)
        place = jnp.where(slot < counts[d], (fbin * 2 + half) * windows + start + slot, -1)
        select = jnp.where(row == place, 1.0, 0.0).astype(jnp.bfloat16)
        for p in range(parts):
            rows = pieces[d][:slots, p * 2 * bins:(p + 1) * 2 * bins].reshape(in_rows, chan)
            packed[p] += jnp.dot(select, rows, preferred_element_type=jnp.float32)
    for p in range(parts):
        block = packed[p].astype(jnp.bfloat16).reshape(bins, 2 * windows, chan)
        packed_ref[p * bins:(p + 1) * bins] = block
        again_ref[p * bins:(p + 1) * bins] = block


def pack_windows(me, pieces, held, parts, windows):
    slots, chan = pieces[0].shape[0] - 1, pieces[0].shape[2]
    nodes = len(pieces)
    bins = pieces[0].shape[1] // (2 * parts)
    whole = pl.BlockSpec(memory_space=pltpu.VMEM)
    anywhere = pl.BlockSpec(memory_space=pl.ANY)
    packed = jax.ShapeDtypeStruct((parts * bins, 2 * windows, chan), jnp.bfloat16)

    def kernel(me_ref, *refs):
        outs = refs[nodes + len(held):]
        pack_kernel(nodes, slots, parts, bins, windows, me_ref, *refs[:nodes], *outs[:2])

    result = pl.pallas_call(
        kernel,
        in_specs=[pl.BlockSpec(memory_space=pltpu.SMEM)] + [whole] * nodes + [anywhere] * len(held),
        out_specs=[whole] * 2 + [anywhere] * len(held),
        out_shape=[packed] * 2 + [jax.ShapeDtypeStruct(array.shape, array.dtype) for array in held],
        input_output_aliases={1 + nodes + k: 2 + k for k in range(len(held))},
        compiler_params=pltpu.CompilerParams(vmem_limit_bytes=VMEM_LIMIT),
        cost_estimate=pl.CostEstimate(flops=1 << 10, bytes_accessed=1 << 10, transcendentals=0),
        name="pack",
    )(me, *pieces, *held)
    return result[0], result[1], list(result[2:])


def conjugate_rows(block):
    depth, chan = block.shape
    i = lax.broadcasted_iota(jnp.int32, (depth, depth), 0)
    j = lax.broadcasted_iota(jnp.int32, (depth, depth), 1)
    half = depth // 2
    swap = jnp.where(i == j + half, 1.0, jnp.where(j == i + half, -1.0, 0.0)).astype(jnp.bfloat16)
    rows = jnp.transpose(block, (1, 0))
    return rows, jnp.dot(rows, swap, preferred_element_type=jnp.float32).astype(jnp.bfloat16)


def pairs_body(first, scale, place_ref, ours_ref, theirs_ref, *refs):
    out_ref, rows_ref = refs if first else refs[::-1]
    core = place_ref[0] % 2
    count, _, chan = ours_ref.shape
    for b in range(count):
        if first:
            rows_ref[b, :chan], rows_ref[b, chan:] = conjugate_rows(ours_ref[b])
        ours, theirs = ours_ref[b], theirs_ref[b]
        both = jnp.concatenate(
            [jnp.where(core == 0, ours, theirs), jnp.where(core == 0, theirs, ours)], axis=1
        )
        product = jnp.dot(rows_ref[b], both, preferred_element_type=jnp.float32) * scale
        product = product.astype(jnp.bfloat16)
        out_ref[0, b] = product[:chan]
        out_ref[1, b] = product[chan:]


def pair_products(place, ours, theirs, rows, out, held, bins, groups, first_bin, t, scale):
    chunk_bins, depth, chan = ours.shape
    steps = groups // 2
    per_step = math.gcd(math.gcd(chunk_bins, first_bin), 4)
    block = pl.BlockSpec((per_step, depth, chan), lambda i, p: (i, 0, 0))
    rows_spec = pl.BlockSpec((per_step, 2 * chan, depth), lambda i, p: (i, 0, 0))
    anywhere = pl.BlockSpec(memory_space=pl.ANY)
    first = rows is None
    operands, specs = [place, ours, theirs], [block, block]
    if not first:
        operands.append(rows)
        specs.append(rows_spec)
    out_spec = pl.BlockSpec(
        (2, per_step, chan, 2 * chan),
        lambda i, p: (0, first_bin // per_step + i, 0, lax.rem(p[0] // 2 - t + steps, steps)),
    )
    out_specs, out_shape = [], []
    aliases = {}
    if out is not None:
        aliases[len(operands)] = 0
        operands.append(out)
        specs.append(anywhere)
    out_specs.append(out_spec)
    out_shape.append(jax.ShapeDtypeStruct((2, bins, chan, groups * chan), jnp.bfloat16))
    if first:
        out_specs.append(rows_spec)
        out_shape.append(jax.ShapeDtypeStruct((chunk_bins, 2 * chan, depth), jnp.bfloat16))
    for array in held:
        aliases[len(operands)] = len(out_specs)
        operands.append(array)
        specs.append(anywhere)
        out_specs.append(anywhere)
        out_shape.append(jax.ShapeDtypeStruct(array.shape, array.dtype))

    def kernel(place_ref, *refs):
        ins, outs = refs[:len(specs)], refs[len(specs):]
        inner = ins[:2] + (outs[:2] if first else (ins[2], outs[0]))
        pairs_body(first, scale, place_ref, *inner)

    result = pl.pallas_call(
        kernel,
        grid_spec=pltpu.PrefetchScalarGridSpec(
            num_scalar_prefetch=1, grid=(chunk_bins // per_step,), in_specs=specs, out_specs=out_specs
        ),
        out_shape=out_shape,
        input_output_aliases=aliases,
        compiler_params=pltpu.CompilerParams(vmem_limit_bytes=VMEM_LIMIT),
        cost_estimate=pl.CostEstimate(flops=1 << 10, bytes_accessed=1 << 10, transcendentals=0),
        name="pairs",
    )(*operands)
    rows = result[1] if first else rows
    return result[0], rows, result[len(result) - len(held):]


def tie(arrays):
    anywhere = pl.BlockSpec(memory_space=pl.ANY)
    return pl.pallas_call(
        lambda *refs: None,
        in_specs=[anywhere] * len(arrays),
        out_specs=[anywhere] * len(arrays),
        out_shape=[jax.ShapeDtypeStruct(array.shape, array.dtype) for array in arrays],
        input_output_aliases={k: k for k in range(len(arrays))},
        compiler_params=pltpu.CompilerParams(vmem_limit_bytes=1 << 20),
        cost_estimate=pl.CostEstimate(flops=1, bytes_accessed=1, transcendentals=0),
        name="tie",
    )(*arrays)


def shards(nodes, groups, segments, available, node_windows):
    slots, chan, samples = segments.shape
    bins = FREQS // nodes
    part_bins = math.gcd(bins, PART_BINS)
    parts = CHUNK_PARTS.get(bins // part_bins, [1] * (bins // part_bins))
    starts = [sum(parts[:c]) * part_bins for c in range(len(parts))]
    chunks = len(parts)
    windows = slots * nodes * 5 // 8
    steps = groups // 2
    me = lax.axis_index("freq").astype(jnp.int32).reshape(1)
    place = lax.axis_index("chan").astype(jnp.int32).reshape(1)
    swap = [[(f, f ^ d) for f in range(nodes)] for d in range(nodes)]
    ring = [(i, (i + 2) % groups) for i in range(groups)]
    cores = [(i, i ^ 1) for i in range(groups)]

    table = jnp.asarray(transform_table(nodes, part_bins, samples))
    pieces = spectra_pieces(
        me, node_windows, segments, available, table, [2 * part_bins * count for count in parts]
    )
    ours, theirs, rows, travelling = {}, {}, {}, {}
    out = None
    scale = 1.0 / windows

    def meet(c, t):
        theirs[c, t] = lax.ppermute(ours[c, t], "chan", cores)

    def send(c, t):
        travelling[c, t] = lax.ppermute(travelling[c, t - 1], "chan", ring)

    def multiply(c, t, held=()):
        nonlocal out
        out, rows[c], kept = pair_products(
            place, ours[c, t], theirs[c, t], rows.get(c), out, list(held), bins, groups, starts[c], t, scale
        )
        return list(kept)

    for c in reversed(range(chunks)):
        exchanged = [pieces[c][0]] + [lax.ppermute(pieces[c][d], "freq", swap[d]) for d in range(1, nodes)]
        held = []
        travelling[c, 0], ours[c, 0], kept = pack_windows(me, exchanged, held, parts[c], windows)
        if held:
            pieces[c + 1][-1:] = kept

    order = RING if chunks == 2 and steps == 4 else [(c, t) for t in range(1, steps) for c in range(chunks)]
    sent = 0

    def launch(done):
        nonlocal sent
        while sent < len(order) and sent < done + DEPTH:
            c, t = order[sent]
            if t > 1 and order.index((c, t - 1)) >= done:
                return
            send(c, t)
            sent += 1

    launch(0)
    meet(0, 0)
    multiply(0, 0)
    ready = []
    if chunks > 1:
        meet(1, 0)
        ready.append((1, 0))
    for k, now in enumerate(order):
        if ready and k + 1 < len(order):
            (travelling[now],) = multiply(*ready.pop(0), [travelling[now]])
        elif ready:
            while len(ready) > 1:
                multiply(*ready.pop(0))
            c, t = ready.pop(0)
            half = ours[c, t].shape[0] // 2
            for b in (0, half):
                mine = ours[c, t][b:b + half]
                out, _, _ = pair_products(
                    place, mine, lax.ppermute(mine, "chan", cores), rows[c][b:b + half], out, [],
                    bins, groups, starts[c] + b, t, scale,
                )
            travelling[now], out = tie([travelling[now], out])
        ours[now] = travelling[now]
        launch(k + 1)
        if k + 2 != len(order) or chunks < 2:
            meet(*now)
        ready.append(now)
        if now[1] == 1 and now[0] not in rows and (now[0], 0) not in ready:
            meet(now[0], 0)
            multiply(now[0], 0)
    while ready:
        multiply(*ready.pop(0))
    return out


def solution(mesh):
    placed = (P("freq", "chan", None), P("freq", "chan"), P("freq"))
    return jax.shard_map(
        functools.partial(shards, mesh.shape["freq"], mesh.shape["chan"]),
        mesh=mesh,
        in_specs=placed,
        out_specs=P(None, "freq", "chan", None),
        check_vma=False,
    )
```
